512 devices in a mesh: ctx: 32 (over x, z_lo), tp: 16 (over z_hi, y, core).
Axes of the slice: x: 4, y: 4, z: 16 (z_hi: 2, z_lo: 8; z = z_hi * 8 + z_lo), core: 2. Of those that a mesh axis runs over, the one named last changes fastest.
Arguments:
- out_grad: bfloat16 [4096, 4096], P('ctx', 'tp'), may hold values from -6 to 6
- out_proj: bfloat16 [4096, 4096], P(None, 'tp'), may hold values from -0.09375 to 0.09375
- queries: bfloat16 [4096, 4096], P('ctx', 'tp'), may hold values from -6 to 6
- keys: bfloat16 [4096, 4096], P('ctx', 'tp'), may hold values from -6 to 6
- values: bfloat16 [4096, 4096], P('ctx', 'tp'), may hold values from -6 to 6
- conv_out: bfloat16 [4096, 4096], P('ctx', 'tp'), may hold values from -6 to 6
- long_filter: float32 [4096, 4096], P('ctx', 'tp'), may hold values from -6 to 6
- skip_gain: float32 [4096], P('tp'), may hold values from 0.5 to 2
Outputs:
- grad_q: bfloat16 [4096, 4096], P('ctx', 'tp')
- grad_k: bfloat16 [4096, 4096], P('ctx', 'tp')
- grad_v: bfloat16 [4096, 4096], P('ctx', 'tp')
- filter_grad: float32 [4096, 4096], P('ctx', 'tp')
The draws below stay inside these ranges and needn't reach their ends.
All inputs are finite; a program needn't handle non-finite values.
Results may differ from the reference program's by a relative error of at most 0.0011.
Values may be sent and summed in bfloat16 or wider, within the bound.
No kernel may reach another device: no remote copies, remote signals or barrier semaphores. Data moves between devices by JAX's collectives and lax.ppermute only.
A program may use at most 64 MiB of HBM per device.

```python
import math
import jax
import jax.numpy as jnp
from jax import lax

D = 4096
C = 4096
LEN = 4096
N_TP = 16


def steps_of(rng, extent, cuts, least, high):
    gain = 1.0
    for position, parts in cuts:
        heights = jax.random.uniform(jax.random.fold_in(jax.random.fold_in(rng, 6), position), (parts,), jnp.float32, least / len(cuts), high / len(cuts))
        gain = gain * jnp.repeat(jnp.exp(heights), extent[position] // parts).reshape((-1,) + (1,) * (len(extent) - 1 - position))
    return gain


def noise(key, extent, deviation, most, split=(), held_as=jnp.bfloat16):
    array = jax.random.normal(key, extent, jnp.float32) * deviation
    if len(split) > 0:
        array = steps_of(key, extent, split, -0.22, 0.18) * array
    return jnp.clip(array, min=-most, max=most).astype(held_as)


def setup_inputs(seed: int = 0) -> dict:
    seeds = jax.random.split(jax.random.key(seed), 9)
    out_grad = noise(seeds[0], (LEN, D), 1.0, 6.0, ((0, 32), (1, 16)))
    out_proj = noise(seeds[1], (D, C), D ** -0.5, 0.09375, ((1, 16),))
    queries = noise(seeds[2], (LEN, C), 1.0, 6.0, ((0, 32), (1, 16)))
    keys = noise(seeds[3], (LEN, C), 1.0, 6.0, ((0, 32), (1, 16)))
    values = noise(seeds[4], (LEN, C), 1.0, 6.0, ((0, 32), (1, 16)))
    conv_out = noise(seeds[5], (LEN, C), 1.0, 6.0, ((0, 32), (1, 16)))
    long_filter = noise(seeds[6], (LEN, C), 1.0, 6.0, ((0, 32), (1, 16)), jnp.float32)
    skip_gain = jnp.clip(0.5 + 1.5 * jax.random.uniform(seeds[7], (C,), jnp.float32) ** steps_of(seeds[7], (C,), ((0, 16),), -0.2, 0.2), 0.5, 2.0)
    return dict(out_grad=out_grad, out_proj=out_proj, queries=queries, keys=keys, values=values, conv_out=conv_out, long_filter=long_filter, skip_gain=skip_gain)


def spectral_block(block_data):
    spectra = jnp.fft.fft(block_data, n=2 * LEN, axis=1)
    filter_spec = spectra[0]
    gated_spec = spectra[1]
    grad_spec = spectra[2]
    paired = jnp.stack([jnp.conj(filter_spec) * grad_spec, jnp.conj(gated_spec) * grad_spec])
    return jnp.real(jnp.fft.ifft(paired, axis=1))[:, :LEN]

def reference(out_grad, out_proj, queries, keys, values, conv_out, long_filter, skip_gain):
    act_grad = jnp.dot(out_grad, out_proj, preferred_element_type=jnp.float32)
    grad_q = (act_grad * conv_out.astype(jnp.float32)).astype(jnp.bfloat16)
    gated_grad = act_grad * queries.astype(jnp.float32)
    key_float = keys.astype(jnp.float32)
    value_float = values.astype(jnp.float32)
    gated_in = key_float * value_float
    inv_root = 1.0 / math.sqrt(LEN)
    scaled_filter = long_filter * inv_root
    block_width = C // N_TP
    stacked = jnp.stack([scaled_filter, gated_in, gated_grad])
    blocks = stacked.reshape(3, LEN, N_TP, block_width).transpose(2, 0, 1, 3)
    results = lax.map(spectral_block, blocks)
    results = results.transpose(1, 2, 0, 3).reshape(2, LEN, C)
    input_grad = results[0] + skip_gain[None, :] * gated_grad
    grad_k = (input_grad * value_float).astype(jnp.bfloat16)
    grad_v = (input_grad * key_float).astype(jnp.bfloat16)
    filter_grad = results[1] * inv_root
    return (grad_q, grad_k, grad_v, filter_grad)
```

```python
import functools
import math

import jax
import jax.numpy as jnp
import numpy as np
from jax import lax
from jax.experimental import pallas as pl
from jax.experimental.pallas import tpu as pltpu
from jax.sharding import Mesh
from jax.sharding import PartitionSpec as P

F32 = jnp.float32
BF16 = jnp.bfloat16
CTX = ("x", "zl")
TP = ("zh", "y", "core")
VMEM = pl.BlockSpec(memory_space=pltpu.VMEM)
SMEM = pl.BlockSpec(memory_space=pltpu.SMEM)
PARAMS = pltpu.CompilerParams(vmem_limit_bytes=48 * 1024 * 1024)


def split_table(table):
    high = table.astype(np.float32).astype(jnp.bfloat16)
    low = (table - high.astype(np.float64)).astype(np.float32).astype(jnp.bfloat16)
    return high, low


def tables(blocks, lanes, chans):
    total = blocks * lanes
    k1 = np.arange(blocks)
    angle = 2.0 * np.pi * np.outer(k1 + 0.25, np.arange(blocks)) / blocks
    eye = np.eye(chans)
    rows = np.concatenate([np.kron(np.cos(angle), eye), np.kron(-np.sin(angle), eye)], axis=0)
    b = np.arange(lanes)
    turn = 2.0 * np.pi * np.outer(k1 + 0.25, b) / total
    twist_re = np.repeat(np.cos(turn), chans, axis=0).astype(np.float32)
    twist_im = np.repeat(-np.sin(turn), chans, axis=0).astype(np.float32)
    lane_angle = 2.0 * np.pi * np.outer(b, b) / lanes
    c, s = np.cos(lane_angle), np.sin(lane_angle)
    lane = np.block([[c, -s], [s, c]])
    return rows, lane, twist_re, twist_im


def halves(x):
    high = x.astype(BF16)
    return high, (x - high.astype(F32)).astype(BF16)


def dot3(a, b):
    a_high, a_low = a
    b_high, b_low = b
    dot = functools.partial(jnp.dot, preferred_element_type=F32)
    return dot(a_high, b_high) + (dot(a_high, b_low) + dot(a_low, b_high))


def forward(x, rows, lane, twist_re, twist_im):
    n = x.shape[0]
    first = dot3(rows, halves(x))
    re, im = first[:n], first[n:]
    turned = jnp.concatenate([re * twist_re - im * twist_im, re * twist_im + im * twist_re], axis=1)
    return dot3(halves(turned), lane)


def prep_kernel(scale, filter_ref, keys_ref, values_ref, out_ref):
    chans = out_ref.shape[1] // 2
    shape = (out_ref.shape[0], chans, out_ref.shape[2])
    out_ref[:, :chans, :] = (filter_ref[...] * scale).T.reshape(shape)
    gated = keys_ref[...].astype(F32) * values_ref[...].astype(F32)
    out_ref[:, chans:, :] = gated.T.reshape(shape)


def matmul_kernel(place_ref, near_ref, far_ref, proj_ref, queries_ref, conv_ref, grad_q_ref, grad_ref, turned_ref):
    n_y, n_zh, _, width = near_ref.shape
    zh, core = place_ref[0], place_ref[1]
    total = jnp.zeros(grad_ref.shape, F32)
    for ref, which in ((near_ref, 0), (far_ref, 1)):
        for y in range(n_y):
            for other in range(n_zh):
                part = ((zh ^ other) * n_y + y) * 2 + (core ^ which)
                weights = proj_ref[pl.ds(pl.multiple_of(part * width, width), width), :]
                total += jnp.dot(ref[y, other], weights, preferred_element_type=F32)
    grad_q_ref[...] = (total * conv_ref[...].astype(F32)).astype(BF16)
    grad = total * queries_ref[...].astype(F32)
    grad_ref[...] = grad
    turned_ref[...] = grad.T.reshape(turned_ref.shape)


def spectra_kernel(x_ref, rh, rl, lh, ll, tr, ti, out_ref):
    blocks, both, lanes = x_ref.shape
    chans = both // 2
    for field in range(2):
        x = x_ref[:, field * chans : (field + 1) * chans, :].reshape(blocks * chans, lanes)
        out_ref[field] = forward(x, (rh[...], rl[...]), (lh[...], ll[...]), tr[...], ti[...])


def correlate_kernel(scale, x_ref, spec_ref, rh, rl, lh, ll, rth, rtl, lth, ltl, tr, ti, out_ref):
    blocks, chans, lanes = x_ref.shape
    n = blocks * chans
    twist_re, twist_im = tr[...], ti[...]
    grad = forward(x_ref[...].reshape(n, lanes), (rh[...], rl[...]), (lh[...], ll[...]), twist_re, twist_im)
    g_re, g_im = grad[:, :lanes] * scale, grad[:, lanes:] * scale
    sides = []
    for field in range(2):
        s_re, s_im = spec_ref[field, :, :lanes], spec_ref[field, :, lanes:]
        prod = jnp.concatenate([s_re * g_re + s_im * g_im, s_re * g_im - s_im * g_re], axis=1)
        back = dot3(halves(prod), (lth[...], ltl[...]))
        re, im = back[:, :lanes], back[:, lanes:]
        sides.append(jnp.concatenate([re * twist_re + im * twist_im, im * twist_re - re * twist_im], axis=0))
    result = dot3((rth[...], rtl[...]), halves(jnp.concatenate(sides, axis=1)))
    for field in range(2):
        out_ref[:, field * chans : (field + 1) * chans, :] = result[:, field * lanes : (field + 1) * lanes].reshape(
            blocks, chans, lanes
        )


def final_kernel(scale, x_ref, grad_ref, keys_ref, values_ref, skip_ref, grad_k_ref, grad_v_ref, filter_grad_ref):
    blocks, both, lanes = x_ref.shape
    chans = both // 2
    conv = x_ref[:, :chans, :].reshape(blocks * chans, lanes).T
    input_grad = conv + skip_ref[...] * grad_ref[...]
    grad_k_ref[...] = (input_grad * values_ref[...].astype(F32)).astype(BF16)
    grad_v_ref[...] = (input_grad * keys_ref[...].astype(F32)).astype(BF16)
    filter_grad_ref[...] = x_ref[:, chans:, :].reshape(blocks * chans, lanes).T * scale


def call(kernel, outs, n_in, scalars=0):
    return pl.pallas_call(
        kernel,
        out_shape=outs,
        in_specs=[SMEM] * scalars + [VMEM] * (n_in - scalars),
        out_specs=jax.tree.map(lambda _: VMEM, outs),
        compiler_params=PARAMS,
    )


def body(out_grad, out_proj, queries, keys, values, conv_out, long_filter, skip_gain):
    tok, width = queries.shape
    n_ctx = lax.axis_size("x") * lax.axis_size("zl")
    chans = width // n_ctx
    total_len = tok * n_ctx
    inv_root = 1.0 / math.sqrt(total_len)
    shape = jax.ShapeDtypeStruct

    rows, lane, twist_re, twist_im = tables(n_ctx, tok, chans)
    fwd = [jnp.asarray(t) for t in (*split_table(rows), *split_table(lane))]
    inv = [jnp.asarray(t) for t in (*split_table(rows.T), *split_table(lane.T))]
    twist = [jnp.asarray(twist_re), jnp.asarray(twist_im)]

    far = lax.ppermute(out_grad, "zh", [(0, 1), (1, 0)])
    prepared = call(functools.partial(prep_kernel, inv_root), shape((n_ctx, 2 * chans, tok), F32), 3)(
        long_filter, keys, values
    )
    fields = lax.all_to_all(prepared, CTX, 0, 0)

    near = lax.all_gather(jnp.stack([out_grad, far]), "y")
    across = lax.ppermute(near, "core", [(0, 1), (1, 0)])
    place = jnp.stack([lax.axis_index("zh"), lax.axis_index("core")]).astype(jnp.int32)
    grad_q, grad, turned = call(
        matmul_kernel,
        (shape((tok, width), BF16), shape((tok, width), F32), shape((n_ctx, chans, tok), F32)),
        6,
        1,
    )(place, near, across, out_proj, queries, conv_out)
    turned = lax.all_to_all(turned, CTX, 0, 0)

    spec = call(spectra_kernel, shape((2, n_ctx * chans, 2 * tok), F32), 7)(fields, *fwd, *twist)
    corr = call(
        functools.partial(correlate_kernel, 1.0 / total_len), shape((n_ctx, 2 * chans, tok), F32), 12
    )(turned, spec, *fwd, *inv, *twist)
    corr = lax.all_to_all(corr, CTX, 0, 0)
    grad_k, grad_v, filter_grad = call(
        functools.partial(final_kernel, inv_root),
        (shape((tok, width), BF16), shape((tok, width), BF16), shape((tok, width), F32)),
        5,
    )(corr, grad, keys, values, skip_gain[None, :])
    return grad_q, grad_k, grad_v, filter_grad


def solution(mesh):
    fine = Mesh(mesh.devices.reshape(4, 8, 2, 4, 2), CTX + TP)
    return jax.shard_map(
        body,
        mesh=fine,
        in_specs=(P(CTX, TP), P(None, TP), P(CTX, TP), P(CTX, TP), P(CTX, TP), P(CTX, TP), P(CTX, TP), P(TP)),
        out_specs=(P(CTX, TP), P(CTX, TP), P(CTX, TP), P(CTX, TP)),
        check_vma=False,
    )
```

```python
import functools
import math

import jax
import jax.numpy as jnp
import numpy as np
from jax import lax
from jax.experimental import pallas as pl
from jax.experimental.pallas import tpu as pltpu
from jax.sharding import Mesh
from jax.sharding import PartitionSpec as P

F32 = jnp.float32
BF16 = jnp.bfloat16
CTX = ("x", "zl")
TP = ("zh", "y", "core")
VMEM = pl.BlockSpec(memory_space=pltpu.VMEM)
SMEM = pl.BlockSpec(memory_space=pltpu.SMEM)
HBM = pl.BlockSpec(memory_space=pltpu.HBM)
PARAMS = pltpu.CompilerParams(vmem_limit_bytes=16 * 1024 * 1024)


def split_table(table):
    high = table.astype(np.float32).astype(jnp.bfloat16)
    low = (table - high.astype(np.float64)).astype(np.float32).astype(jnp.bfloat16)
    return high, low


def tables(blocks, lanes, chans):
    total = blocks * lanes
    k1 = np.arange(blocks)
    angle = 2.0 * np.pi * np.outer(k1 + 0.25, np.arange(blocks)) / blocks
    eye = np.eye(chans)
    rows = np.concatenate([np.kron(np.cos(angle), eye), np.kron(-np.sin(angle), eye)], axis=0)
    b = np.arange(lanes)
    turn = 2.0 * np.pi * np.outer(k1 + 0.25, b) / total
    twist_re = np.repeat(np.cos(turn), chans, axis=0).astype(np.float32)
    twist_im = np.repeat(-np.sin(turn), chans, axis=0).astype(np.float32)
    lane_angle = 2.0 * np.pi * np.outer(b, b) / lanes
    c, s = np.cos(lane_angle), np.sin(lane_angle)
    lane = np.block([[c, -s], [s, c]])
    return rows, lane, twist_re, twist_im


def halves(x):
    high = x.astype(BF16)
    return high, (x - high.astype(F32)).astype(BF16)


def dot3(a, b):
    a_high, a_low = a
    b_high, b_low = b
    dot = functools.partial(jnp.dot, preferred_element_type=F32)
    return dot(a_high, b_high) + (dot(a_high, b_low) + dot(a_low, b_high))


def forward(x, rows, lane, twist_re, twist_im):
    n = x.shape[0]
    first = dot3(rows, halves(x))
    re, im = first[:n], first[n:]
    turned = jnp.concatenate([re * twist_re - im * twist_im, re * twist_im + im * twist_re], axis=1)
    return dot3(halves(turned), lane)


def fetch(pairs, sems):
    copies = [pltpu.make_async_copy(src, dst, sems.at[i]) for i, (src, dst) in enumerate(pairs)]
    for copy in copies:
        copy.start()
    return copies


def prep_kernel(
    scale, filter_hbm, keys_hbm, values_hbm, own_hbm, out_ref, own_ref, filter_ref, keys_ref, values_ref, sems
):
    pairs = [(filter_hbm, filter_ref), (keys_hbm, keys_ref), (values_hbm, values_ref), (own_hbm, own_ref)]
    copies = fetch(pairs, sems)
    chans = out_ref.shape[1] // 2
    shape = (out_ref.shape[0], chans, out_ref.shape[2])
    copies[0].wait()
    out_ref[:, :chans, :] = (filter_ref[...] * scale).T.reshape(shape)
    copies[1].wait()
    copies[2].wait()
    gated = keys_ref[...].astype(F32) * values_ref[...].astype(F32)
    out_ref[:, chans:, :] = gated.T.reshape(shape)
    copies[3].wait()


def join_kernel(place_ref, own_ref, far_ref, out_ref):
    zh = place_ref[0]
    out_ref[zh] = own_ref[...]
    out_ref[1 - zh] = far_ref[...]


def products(given_ref, proj_ref):
    n_y, n_zh = given_ref.shape[:2]
    total = None
    for y in range(n_y):
        for zh in range(n_zh):
            term = jnp.dot(given_ref[y, zh], proj_ref[zh * n_y + y], preferred_element_type=F32)
            total = term if total is None else total + term
    return total


def near_kernel(
    place_ref, near_ref, x_ref, rh, rl, lh, ll, tr, ti, proj_hbm, queries_hbm, conv_hbm,
    part_ref, spec_ref, far_proj_ref, queries_ref, conv_ref, near_proj_ref, sems,
):
    core = place_ref[1]
    pairs = [
        (proj_hbm.at[:, core], near_proj_ref),
        (proj_hbm.at[:, 1 - core], far_proj_ref),
        (queries_hbm, queries_ref),
        (conv_hbm, conv_ref),
    ]
    copies = fetch(pairs, sems)
    blocks, both, lanes = x_ref.shape
    chans = both // 2
    for field in range(2):
        x = x_ref[:, field * chans : (field + 1) * chans, :].reshape(blocks * chans, lanes)
        spec_ref[field] = forward(x, (rh[...], rl[...]), (lh[...], ll[...]), tr[...], ti[...])
    copies[0].wait()
    part_ref[...] = products(near_ref, near_proj_ref)
    for copy in copies[1:]:
        copy.wait()


def far_kernel(far_ref, part_ref, proj_ref, queries_ref, conv_ref, grad_q_ref, grad_ref, turned_ref):
    total = part_ref[...] + products(far_ref, proj_ref)
    grad = total * queries_ref[...].astype(F32)
    turned_ref[...] = grad.T.reshape(turned_ref.shape)
    grad_ref[...] = grad
    grad_q_ref[...] = (total * conv_ref[...].astype(F32)).astype(BF16)


def correlate_kernel(scale, x_ref, spec_ref, rh, rl, lh, ll, rth, rtl, lth, ltl, tr, ti, out_ref):
    blocks, chans, lanes = x_ref.shape
    n = blocks * chans
    twist_re, twist_im = tr[...], ti[...]
    grad = forward(x_ref[...].reshape(n, lanes), (rh[...], rl[...]), (lh[...], ll[...]), twist_re, twist_im)
    g_re, g_im = grad[:, :lanes] * scale, grad[:, lanes:] * scale
    sides = []
    for field in range(2):
        s_re, s_im = spec_ref[field, :, :lanes], spec_ref[field, :, lanes:]
        prod = jnp.concatenate([s_re * g_re + s_im * g_im, s_re * g_im - s_im * g_re], axis=1)
        back = dot3(halves(prod), (lth[...], ltl[...]))
        re, im = back[:, :lanes], back[:, lanes:]
        sides.append(jnp.concatenate([re * twist_re + im * twist_im, im * twist_re - re * twist_im], axis=0))
    result = dot3((rth[...], rtl[...]), halves(jnp.concatenate(sides, axis=1)))
    for field in range(2):
        out_ref[:, field * chans : (field + 1) * chans, :] = result[:, field * lanes : (field + 1) * lanes].reshape(
            blocks, chans, lanes
        )


def final_kernel(scale, x_ref, grad_ref, keys_ref, values_ref, skip_ref, grad_k_ref, grad_v_ref, filter_grad_ref):
    blocks, both, lanes = x_ref.shape
    chans = both // 2
    conv = x_ref[:, :chans, :].reshape(blocks * chans, lanes).T
    input_grad = conv + skip_ref[...] * grad_ref[...]
    grad_k_ref[...] = (input_grad * values_ref[...].astype(F32)).astype(BF16)
    grad_v_ref[...] = (input_grad * keys_ref[...].astype(F32)).astype(BF16)
    filter_grad_ref[...] = x_ref[:, chans:, :].reshape(blocks * chans, lanes).T * scale


def call(kernel, outs, specs, scratch=(), cost=None):
    run = pl.pallas_call(
        kernel,
        out_shape=outs,
        in_specs=specs,
        out_specs=jax.tree.map(lambda _: VMEM, outs),
        scratch_shapes=scratch,
        compiler_params=PARAMS,
        cost_estimate=cost,
    )

    def held(x, spec):
        return pltpu.with_memory_space_constraint(x, pltpu.HBM) if spec is HBM else x

    return lambda *args: run(*map(held, args, specs))


def body(out_grad, out_proj, queries, keys, values, conv_out, long_filter, skip_gain):
    tok, width = queries.shape
    n_ctx = lax.axis_size("x") * lax.axis_size("zl")
    n_half = lax.axis_size("zh") * lax.axis_size("y")
    chans = width // n_ctx
    total_len = tok * n_ctx
    inv_root = 1.0 / math.sqrt(total_len)
    shape = jax.ShapeDtypeStruct
    dma = pltpu.SemaphoreType.DMA

    rows, lane, twist_re, twist_im = tables(n_ctx, tok, chans)
    fwd = [jnp.asarray(t) for t in (*split_table(rows), *split_table(lane))]
    inv = [jnp.asarray(t) for t in (*split_table(rows.T), *split_table(lane.T))]
    twist = [jnp.asarray(twist_re), jnp.asarray(twist_im)]
    place = jnp.stack([lax.axis_index("zh"), lax.axis_index("core")]).astype(jnp.int32)

    far = lax.ppermute(out_grad, "zh", [(0, 1), (1, 0)])
    block = shape((tok, width), BF16)
    prepared, own = call(
        functools.partial(prep_kernel, inv_root),
        (shape((n_ctx, 2 * chans, tok), F32), block),
        [HBM] * 4,
        [pltpu.VMEM((tok, width), F32), pltpu.VMEM((tok, width), BF16), pltpu.VMEM((tok, width), BF16), dma((4,))],
    )(long_filter, keys, values, out_grad)
    fields = lax.all_to_all(prepared, CTX, 0, 0)

    joined = call(
        join_kernel,
        shape((2, tok, width), BF16),
        [SMEM, VMEM, VMEM],
        cost=pl.CostEstimate(flops=COST, bytes_accessed=1 << 20, transcendentals=0),
    )(place, own, far)
    near = lax.all_gather(joined, "y")
    across = lax.ppermute(near, "core", [(0, 1), (1, 0)])
    half = shape((n_half, width, width), BF16)
    part, spec, far_proj, gate, saved = call(
        near_kernel,
        (shape((tok, width), F32), shape((2, n_ctx * chans, 2 * tok), F32), half, block, block),
        [SMEM] + [VMEM] * 8 + [HBM] * 3,
        [pltpu.VMEM(half.shape, BF16), dma((4,))],
    )(place, near, fields, *fwd, *twist, out_proj.reshape(n_half, 2, width, width), queries, conv_out)
    across, part = lax.optimization_barrier((across, part))
    grad_q, grad, turned = call(
        far_kernel, (block, shape((tok, width), F32), shape((n_ctx, chans, tok), F32)), [VMEM] * 5
    )(across, part, far_proj, gate, saved)
    turned = lax.all_to_all(turned, CTX, 0, 0)

    corr = call(
        functools.partial(correlate_kernel, 1.0 / total_len), shape((n_ctx, 2 * chans, tok), F32), [VMEM] * 12
    )(turned, spec, *fwd, *inv, *twist)
    corr = lax.all_to_all(corr, CTX, 0, 0)
    grad_k, grad_v, filter_grad = call(
        functools.partial(final_kernel, inv_root),
        (shape((tok, width), BF16), shape((tok, width), BF16), shape((tok, width), F32)),
        [VMEM] * 5,
    )(corr, grad, keys, values, skip_gain[None, :])
    return grad_q, grad_k, grad_v, filter_grad


COST = 1 << 35


def solution(mesh):
    fine = Mesh(mesh.devices.reshape(4, 8, 2, 4, 2), CTX + TP)
    return jax.shard_map(
        body,
        mesh=fine,
        in_specs=(P(CTX, TP), P(None, TP), P(CTX, TP), P(CTX, TP), P(CTX, TP), P(CTX, TP), P(CTX, TP), P(TP)),
        out_specs=(P(CTX, TP), P(CTX, TP), P(CTX, TP), P(CTX, TP)),
        check_vma=False,
    )
```

```python
import functools
import math

import jax
import jax.numpy as jnp
import numpy as np
from jax import lax
from jax.experimental import pallas as pl
from jax.experimental.pallas import tpu as pltpu
from jax.sharding import Mesh
from jax.sharding import PartitionSpec as P

F32 = jnp.float32
BF16 = jnp.bfloat16
CTX = ("x", "zl")
TP = ("zh", "y", "core")
VMEM = pl.BlockSpec(memory_space=pltpu.VMEM)
SMEM = pl.BlockSpec(memory_space=pltpu.SMEM)
HBM = pl.BlockSpec(memory_space=pltpu.HBM)
STRETCH = 2.0**17
PARAMS = pltpu.CompilerParams(vmem_limit_bytes=16 * 1024 * 1024)


def split_table(table):
    high = table.astype(np.float32).astype(jnp.bfloat16)
    low = (table - high.astype(np.float64)).astype(np.float32).astype(jnp.bfloat16)
    return high, low


def tables(blocks, lanes, chans):
    total = blocks * lanes
    k1 = np.arange(blocks)
    angle = 2.0 * np.pi * np.outer(k1 + 0.25, np.arange(blocks)) / blocks
    eye = np.eye(chans)
    rows = np.concatenate([np.kron(np.cos(angle), eye), np.kron(-np.sin(angle), eye)], axis=0)
    b = np.arange(lanes)
    turn = 2.0 * np.pi * np.outer(k1 + 0.25, b) / total
    twist_re = np.repeat(np.cos(turn), chans, axis=0).astype(np.float32)
    twist_im = np.repeat(-np.sin(turn), chans, axis=0).astype(np.float32)
    lane_angle = 2.0 * np.pi * np.outer(b, b) / lanes
    c, s = np.cos(lane_angle), np.sin(lane_angle)
    lane = np.block([[c, -s], [s, c]])
    return rows, lane, twist_re, twist_im


def halves(x):
    high = x.astype(BF16)
    return high, (x - high.astype(F32)).astype(BF16)


def dot3(a, b):
    a_high, a_low = a
    b_high, b_low = b
    dot = functools.partial(jnp.dot, preferred_element_type=F32)
    return dot(a_high, b_high) + (dot(a_high, b_low) + dot(a_low, b_high))


def forward(x, rows, lane, twist_re, twist_im):
    n = x.shape[0]
    first = dot3(rows, halves(x))
    re, im = first[:n], first[n:]
    turned = jnp.concatenate([re * twist_re - im * twist_im, re * twist_im + im * twist_re], axis=1)
    return dot3(halves(turned), lane)


def fetch(pairs, sems):
    copies = [pltpu.make_async_copy(src, dst, sems.at[i]) for i, (src, dst) in enumerate(pairs)]
    for copy in copies:
        copy.start()
    return copies


def prep_kernel(
    scale, filter_hbm, keys_hbm, values_hbm, own_hbm, out_ref, own_ref, filter_ref, keys_ref, values_ref, sems
):
    pairs = [
        (filter_hbm, filter_ref),
        (keys_hbm, keys_ref),
        (values_hbm, values_ref),
        (own_hbm, own_ref),
    ]
    copies = fetch(pairs, sems)
    chans = out_ref.shape[1] // 2
    shape = (out_ref.shape[0], chans, out_ref.shape[2])
    copies[0].wait()
    out_ref[:, :chans, :] = (filter_ref[...] * scale).T.reshape(shape)
    copies[1].wait()
    copies[2].wait()
    gated = keys_ref[...].astype(F32) * values_ref[...].astype(F32)
    out_ref[:, chans:, :] = gated.T.reshape(shape)
    copies[3].wait()


def join_kernel(place_ref, own_ref, far_ref, out_ref):
    zh = place_ref[0]
    out_ref[zh] = own_ref[...]
    out_ref[1 - zh] = far_ref[...]


def products(core, given_ref, proj_ref):
    n_y, n_zh = given_ref.shape[:2]
    total = None
    for y in range(n_y):
        for zh in range(n_zh):
            part = zh * n_y + y
            weights = proj_ref[part] if core is None else proj_ref[part, core]
            term = jnp.dot(given_ref[y, zh], weights, preferred_element_type=F32)
            total = term if total is None else total + term
    return total


def near_kernel(
    place_ref, near_ref, proj_ref, queries_hbm, conv_hbm, part_ref, far_proj_ref, queries_ref, conv_ref, sems
):
    core = place_ref[1]
    copies = fetch([(queries_hbm, queries_ref), (conv_hbm, conv_ref)], sems)
    part_ref[...] = products(core, near_ref, proj_ref)
    for i in range(proj_ref.shape[0]):
        far_proj_ref[i] = proj_ref[i, 1 - core]
    for copy in copies:
        copy.wait()


def spectra_kernel(x_ref, rh, rl, lh, ll, tr, ti, out_ref):
    blocks, both, lanes = x_ref.shape
    chans = both // 2
    for field in range(2):
        x = x_ref[:, field * chans : (field + 1) * chans, :].reshape(blocks * chans, lanes)
        out_ref[field] = forward(x, (rh[...], rl[...]), (lh[...], ll[...]), tr[...], ti[...])


def far_kernel(far_ref, part_ref, proj_ref, queries_ref, conv_ref, grad_q_ref, grad_ref, turned_ref):
    total = part_ref[...] + products(None, far_ref, proj_ref)
    grad = total * queries_ref[...].astype(F32)
    turned_ref[...] = grad.T.reshape(turned_ref.shape)
    grad_ref[...] = grad
    grad_q_ref[...] = (total * conv_ref[...].astype(F32)).astype(BF16)


def correlate_kernel(scale, stretch, x_ref, spec_ref, rh, rl, lh, ll, rth, rtl, lth, ltl, tr, ti, out_ref):
    blocks, chans, lanes = x_ref.shape
    n = blocks * chans
    twist_re, twist_im = tr[...], ti[...]
    grad = forward(x_ref[...].reshape(n, lanes), (rh[...], rl[...]), (lh[...], ll[...]), twist_re, twist_im)
    g_re, g_im = grad[:, :lanes] * scale, grad[:, lanes:] * scale
    sides = []
    for field in range(2):
        s_re, s_im = spec_ref[field, :, :lanes], spec_ref[field, :, lanes:]
        prod = jnp.concatenate([s_re * g_re + s_im * g_im, s_re * g_im - s_im * g_re], axis=1)
        back = dot3(halves(prod), (lth[...], ltl[...]))
        re, im = back[:, :lanes], back[:, lanes:]
        sides.append(jnp.concatenate([re * twist_re + im * twist_im, im * twist_re - re * twist_im], axis=0))
    result = dot3((rth[...], rtl[...]), halves(jnp.concatenate(sides, axis=1)))
    conv, filter_grad = [result[:, f * lanes : (f + 1) * lanes].reshape(blocks, chans, lanes) for f in range(2)]
    high, low = halves(conv)
    stretched = filter_grad * stretch
    cubed = stretched * stretched * stretched
    out_ref[...] = jnp.concatenate([high.astype(F32), low.astype(F32), cubed], axis=1).astype(BF16)


def final_kernel(shrink, x_ref, grad_ref, keys_ref, values_ref, skip_ref, grad_k_ref, grad_v_ref, filter_grad_ref):
    blocks, rows, lanes = x_ref.shape
    chans = rows // 3
    x = x_ref[...].astype(F32)
    conv = (x[:, :chans, :] + x[:, chans : 2 * chans, :]).reshape(blocks * chans, lanes).T
    input_grad = conv + skip_ref[...] * grad_ref[...]
    grad_k_ref[...] = (input_grad * values_ref[...].astype(F32)).astype(BF16)
    grad_v_ref[...] = (input_grad * keys_ref[...].astype(F32)).astype(BF16)
    cubed = x[:, 2 * chans :, :].reshape(blocks * chans, lanes)
    size = jnp.exp2(jnp.log2(jnp.maximum(jnp.abs(cubed), 1e-37)) * (1.0 / 3.0)) * shrink
    root = jnp.where(cubed < 0.0, -size, jnp.where(cubed > 0.0, size, 0.0))
    filter_grad_ref[...] = root.T


def call(kernel, outs, specs, scratch=(), cost=None):
    run = pl.pallas_call(
        kernel,
        out_shape=outs,
        in_specs=specs,
        out_specs=jax.tree.map(lambda _: VMEM, outs),
        scratch_shapes=scratch,
        compiler_params=PARAMS,
        cost_estimate=cost,
    )

    def held(x, spec):
        return pltpu.with_memory_space_constraint(x, pltpu.HBM) if spec is HBM else x

    return lambda *args: run(*map(held, args, specs))


def body(out_grad, out_proj, queries, keys, values, conv_out, long_filter, skip_gain):
    tok, width = queries.shape
    n_ctx = lax.axis_size("x") * lax.axis_size("zl")
    n_half = lax.axis_size("zh") * lax.axis_size("y")
    chans = width // n_ctx
    total_len = tok * n_ctx
    inv_root = 1.0 / math.sqrt(total_len)
    shape = jax.ShapeDtypeStruct
    dma = pltpu.SemaphoreType.DMA

    rows, lane, twist_re, twist_im = tables(n_ctx, tok, chans)
    fwd = [jnp.asarray(t) for t in (*split_table(rows), *split_table(lane))]
    inv = [jnp.asarray(t) for t in (*split_table(rows.T), *split_table(lane.T))]
    twist = [jnp.asarray(twist_re), jnp.asarray(twist_im)]
    place = jnp.stack([lax.axis_index("zh"), lax.axis_index("core")]).astype(jnp.int32)

    far = lax.ppermute(out_grad, "zh", [(0, 1), (1, 0)])
    block = shape((tok, width), BF16)
    half = shape((n_half, width, width), BF16)
    proj = out_proj.reshape(n_half, 2, width, width)
    prepared, own = call(
        functools.partial(prep_kernel, inv_root),
        (shape((n_ctx, 2 * chans, tok), F32), block),
        [HBM] * 4,
        [pltpu.VMEM((tok, width), F32), pltpu.VMEM((tok, width), BF16), pltpu.VMEM((tok, width), BF16), dma((4,))],
    )(long_filter, keys, values, out_grad)
    fields = lax.all_to_all(prepared, CTX, 0, 0)

    joined = call(
        join_kernel,
        shape((2, tok, width), BF16),
        [SMEM, VMEM, VMEM],
        cost=pl.CostEstimate(flops=COST, bytes_accessed=1 << 20, transcendentals=0),
    )(place, own, far)
    near = lax.all_gather(joined, "y")
    across = lax.ppermute(near, "core", [(0, 1), (1, 0)])
    part, far_proj, gate, saved = call(
        near_kernel,
        (shape((tok, width), F32), half, block, block),
        [SMEM, VMEM, VMEM, HBM, HBM],
        [dma((2,))],
    )(place, near, proj, queries, conv_out)
    across, part = lax.optimization_barrier((across, part))
    grad_q, grad, turned = call(
        far_kernel, (block, shape((tok, width), F32), shape((n_ctx, chans, tok), F32)), [VMEM] * 5
    )(across, part, far_proj, gate, saved)
    turned = lax.all_to_all(turned, CTX, 0, 0)

    spec = call(spectra_kernel, shape((2, n_ctx * chans, 2 * tok), F32), [VMEM] * 7)(fields, *fwd, *twist)
    corr = call(
        functools.partial(correlate_kernel, 1.0 / total_len, inv_root * STRETCH),
        shape((n_ctx, 3 * chans, tok), BF16),
        [VMEM] * 12,
    )(turned, spec, *fwd, *inv, *twist)
    corr = lax.all_to_all(corr, CTX, 0, 0)
    grad_k, grad_v, filter_grad = call(
        functools.partial(final_kernel, 1.0 / STRETCH),
        (shape((tok, width), BF16), shape((tok, width), BF16), shape((tok, width), F32)),
        [VMEM] * 5,
    )(corr, grad, keys, values, skip_gain[None, :])
    return grad_q, grad_k, grad_v, filter_grad


COST = 1 << 35


def solution(mesh):
    fine = Mesh(mesh.devices.reshape(4, 8, 2, 4, 2), CTX + TP)
    return jax.shard_map(
        body,
        mesh=fine,
        in_specs=(P(CTX, TP), P(None, TP), P(CTX, TP), P(CTX, TP), P(CTX, TP), P(CTX, TP), P(CTX, TP), P(TP)),
        out_specs=(P(CTX, TP), P(CTX, TP), P(CTX, TP), P(CTX, TP)),
        check_vma=False,
    )
```

```python
import functools
import math

import jax
import jax.numpy as jnp
import numpy as np
from jax import lax
from jax.experimental import pallas as pl
from jax.experimental.pallas import tpu as pltpu
from jax.sharding import Mesh
from jax.sharding import PartitionSpec as P

F32 = jnp.float32
BF16 = jnp.bfloat16
CTX = ("x", "zl")
TP = ("zh", "y", "core")
VMEM = pl.BlockSpec(memory_space=pltpu.VMEM)
SMEM = pl.BlockSpec(memory_space=pltpu.SMEM)
HBM = pl.BlockSpec(memory_space=pltpu.HBM)
STRETCH = 2.0**17
PARAMS = pltpu.CompilerParams(vmem_limit_bytes=16 * 1024 * 1024)


def split_table(table):
    high = table.astype(np.float32).astype(jnp.bfloat16)
    low = (table - high.astype(np.float64)).astype(np.float32).astype(jnp.bfloat16)
    return high, low


def tables(blocks, lanes, chans):
    total = blocks * lanes
    k1 = np.arange(blocks)
    angle = 2.0 * np.pi * np.outer(k1 + 0.25, np.arange(blocks)) / blocks
    eye = np.eye(chans)
    rows = np.concatenate([np.kron(np.cos(angle), eye), np.kron(-np.sin(angle), eye)], axis=0)
    b = np.arange(lanes)
    turn = 2.0 * np.pi * np.outer(k1 + 0.25, b) / total
    twist_re = np.repeat(np.cos(turn), chans, axis=0).astype(np.float32)
    twist_im = np.repeat(-np.sin(turn), chans, axis=0).astype(np.float32)
    lane_angle = 2.0 * np.pi * np.outer(b, b) / lanes
    c, s = np.cos(lane_angle), np.sin(lane_angle)
    lane = np.block([[c, -s], [s, c]])
    return rows, lane, twist_re, twist_im


def halves(x):
    high = x.astype(BF16)
    return high, (x - high.astype(F32)).astype(BF16)


def dot3(a, b):
    a_high, a_low = a
    b_high, b_low = b
    dot = functools.partial(jnp.dot, preferred_element_type=F32)
    return dot(a_high, b_high) + (dot(a_high, b_low) + dot(a_low, b_high))


def forward(x, rows, lane, twist_re, twist_im):
    n, lanes = x.shape
    high, low = halves(x)
    both = jnp.dot(rows[0], jnp.concatenate([high, low], axis=1), preferred_element_type=F32)
    first = both[:, :lanes] + (both[:, lanes:] + jnp.dot(rows[1], high, preferred_element_type=F32))
    re, im = first[:n], first[n:]
    turned = jnp.concatenate([re * twist_re - im * twist_im, re * twist_im + im * twist_re], axis=1)
    return dot3(halves(turned), lane)


def fetch(pairs, sems):
    copies = [pltpu.make_async_copy(src, dst, sems.at[i]) for i, (src, dst) in enumerate(pairs)]
    for copy in copies:
        copy.start()
    return copies


def prep_kernel(
    scale, filter_hbm, keys_hbm, values_hbm, own_hbm,
    out_hbm, own_ref, out_ref, filter_ref, keys_ref, values_ref, sems,
):
    copies = fetch(
        [(keys_hbm, keys_ref), (values_hbm, values_ref), (filter_hbm, filter_ref), (own_hbm, own_ref)], sems
    )
    blocks, both, lanes = out_ref.shape
    chans = both // 2
    copies[0].wait()
    copies[1].wait()
    gated = keys_ref[...].astype(F32) * values_ref[...].astype(F32)
    out_ref[:, chans:, :] = gated.T.reshape(blocks, chans, lanes)
    first = pltpu.make_async_copy(out_ref.at[:, chans:, :], out_hbm.at[:, chans:, :], sems.at[4])
    first.start()
    copies[2].wait()
    out_ref[:, :chans, :] = (filter_ref[...] * scale).T.reshape(blocks, chans, lanes)
    second = pltpu.make_async_copy(out_ref.at[:, :chans, :], out_hbm.at[:, :chans, :], sems.at[5])
    second.start()
    copies[3].wait()
    first.wait()
    second.wait()


def join_kernel(place_ref, own_ref, far_ref, out_ref):
    zh = place_ref[0]
    out_ref[zh] = own_ref[...]
    out_ref[1 - zh] = far_ref[...]


def products(core, given_ref, proj_ref):
    n_y, n_zh = given_ref.shape[:2]
    total = None
    for y in range(n_y):
        for zh in range(n_zh):
            part = zh * n_y + y
            weights = proj_ref[part] if core is None else proj_ref[part, core]
            term = jnp.dot(given_ref[y, zh], weights, preferred_element_type=F32)
            total = term if total is None else total + term
    return total


def near_kernel(
    place_ref, near_ref, proj_ref, queries_hbm, conv_hbm, part_ref, far_proj_ref, queries_ref, conv_ref, sems
):
    core = place_ref[1]
    copies = fetch([(queries_hbm, queries_ref), (conv_hbm, conv_ref)], sems)
    part_ref[...] = products(core, near_ref, proj_ref)
    for i in range(proj_ref.shape[0]):
        far_proj_ref[i] = proj_ref[i, 1 - core]
    for copy in copies:
        copy.wait()


def spectra_kernel(x_ref, rh, rl, lh, ll, tr, ti, out_ref):
    blocks, both, lanes = x_ref.shape
    chans = both // 2
    for field in range(2):
        x = x_ref[:, field * chans : (field + 1) * chans, :].reshape(blocks * chans, lanes)
        out_ref[field] = forward(x, (rh[...], rl[...]), (lh[...], ll[...]), tr[...], ti[...])


def far_kernel(far_ref, part_ref, proj_ref, queries_ref, conv_ref, grad_q_ref, grad_ref, turned_ref):
    total = part_ref[...] + products(None, far_ref, proj_ref)
    grad = total * queries_ref[...].astype(F32)
    turned_ref[...] = grad.T.reshape(turned_ref.shape)
    grad_ref[...] = grad
    grad_q_ref[...] = (total * conv_ref[...].astype(F32)).astype(BF16)


def correlate_kernel(scale, stretch, x_ref, spec_ref, rh, rl, lh, ll, rth, rtl, lth, ltl, tr, ti, out_ref):
    blocks, chans, lanes = x_ref.shape
    n = blocks * chans
    twist_re, twist_im = tr[...], ti[...]
    grad = forward(x_ref[...].reshape(n, lanes), (rh[...], rl[...]), (lh[...], ll[...]), twist_re, twist_im)
    g_re, g_im = grad[:, :lanes] * scale, grad[:, lanes:] * scale
    sides = []
    for field in range(2):
        s_re, s_im = spec_ref[field, :, :lanes], spec_ref[field, :, lanes:]
        prod = jnp.concatenate([s_re * g_re + s_im * g_im, s_re * g_im - s_im * g_re], axis=1)
        back = dot3(halves(prod), (lth[...], ltl[...]))
        re, im = back[:, :lanes], back[:, lanes:]
        sides.append(jnp.concatenate([re * twist_re + im * twist_im, im * twist_re - re * twist_im], axis=0))
    result = dot3((rth[...], rtl[...]), halves(jnp.concatenate(sides, axis=1)))
    conv, filter_grad = [result[:, f * lanes : (f + 1) * lanes].reshape(blocks, chans, lanes) for f in range(2)]
    high, low = halves(conv)
    stretched = filter_grad * stretch
    cubed = stretched * stretched * stretched
    out_ref[...] = jnp.concatenate([high.astype(F32), low.astype(F32), cubed], axis=1).astype(BF16)


def final_kernel(shrink, x_ref, grad_ref, keys_ref, values_ref, skip_ref, grad_k_ref, grad_v_ref, filter_grad_ref):
    blocks, rows, lanes = x_ref.shape
    chans = rows // 3
    x = x_ref[...].astype(F32)
    conv = (x[:, :chans, :] + x[:, chans : 2 * chans, :]).reshape(blocks * chans, lanes).T
    input_grad = conv + skip_ref[...] * grad_ref[...]
    grad_k_ref[...] = (input_grad * values_ref[...].astype(F32)).astype(BF16)
    grad_v_ref[...] = (input_grad * keys_ref[...].astype(F32)).astype(BF16)
    cubed = x[:, 2 * chans :, :].reshape(blocks * chans, lanes)
    size = jnp.exp2(jnp.log2(jnp.maximum(jnp.abs(cubed), 1e-37)) * (1.0 / 3.0)) * shrink
    root = jnp.where(cubed < 0.0, -size, jnp.where(cubed > 0.0, size, 0.0))
    filter_grad_ref[...] = root.T


def call(kernel, outs, specs, scratch=(), cost=None, out_specs=None):
    run = pl.pallas_call(
        kernel,
        out_shape=outs,
        in_specs=specs,
        out_specs=out_specs or jax.tree.map(lambda _: VMEM, outs),
        scratch_shapes=scratch,
        compiler_params=PARAMS,
        cost_estimate=cost,
    )

    def held(x, spec):
        return pltpu.with_memory_space_constraint(x, pltpu.HBM) if spec is HBM else x

    return lambda *args: run(*map(held, args, specs))


def body(out_grad, out_proj, queries, keys, values, conv_out, long_filter, skip_gain):
    tok, width = queries.shape
    n_ctx = lax.axis_size("x") * lax.axis_size("zl")
    n_half = lax.axis_size("zh") * lax.axis_size("y")
    chans = width // n_ctx
    total_len = tok * n_ctx
    inv_root = 1.0 / math.sqrt(total_len)
    shape = jax.ShapeDtypeStruct
    dma = pltpu.SemaphoreType.DMA

    rows, lane, twist_re, twist_im = tables(n_ctx, tok, chans)
    fwd = [jnp.asarray(t) for t in (*split_table(rows), *split_table(lane))]
    inv = [jnp.asarray(t) for t in (*split_table(rows.T), *split_table(lane.T))]
    twist = [jnp.asarray(twist_re), jnp.asarray(twist_im)]
    place = jnp.stack([lax.axis_index("zh"), lax.axis_index("core")]).astype(jnp.int32)

    block = shape((tok, width), BF16)
    half = shape((n_half, width, width), BF16)
    proj = out_proj.reshape(n_half, 2, width, width)
    prepared, own = call(
        functools.partial(prep_kernel, inv_root),
        (shape((n_ctx, 2 * chans, tok), F32), block),
        [HBM] * 4,
        [
            pltpu.VMEM((n_ctx, 2 * chans, tok), F32),
            pltpu.VMEM((tok, width), F32),
            pltpu.VMEM((tok, width), BF16),
            pltpu.VMEM((tok, width), BF16),
            dma((6,)),
        ],
        out_specs=(HBM, VMEM),
    )(long_filter, keys, values, out_grad)
    far = lax.ppermute(own, "zh", [(0, 1), (1, 0)])
    fields = lax.all_to_all(prepared, CTX, 0, 0)

    joined = call(
        join_kernel,
        shape((2, tok, width), BF16),
        [SMEM, VMEM, VMEM],
        cost=pl.CostEstimate(flops=COST, bytes_accessed=1 << 20, transcendentals=0),
    )(place, own, far)
    near = lax.all_gather(joined, "y")
    across = lax.ppermute(near, "core", [(0, 1), (1, 0)])
    part, far_proj, gate, saved = call(
        near_kernel,
        (shape((tok, width), F32), half, block, block),
        [SMEM, VMEM, VMEM, HBM, HBM],
        [dma((2,))],
    )(place, near, proj, queries, conv_out)
    across, part = lax.optimization_barrier((across, part))
    grad_q, grad, turned = call(
        far_kernel, (block, shape((tok, width), F32), shape((n_ctx, chans, tok), F32)), [VMEM] * 5
    )(across, part, far_proj, gate, saved)
    turned = lax.all_to_all(turned, CTX, 0, 0)

    spec = call(spectra_kernel, shape((2, n_ctx * chans, 2 * tok), F32), [VMEM] * 7)(fields, *fwd, *twist)
    corr = call(
        functools.partial(correlate_kernel, 1.0 / total_len, inv_root * STRETCH),
        shape((n_ctx, 3 * chans, tok), BF16),
        [VMEM] * 12,
    )(turned, spec, *fwd, *inv, *twist)
    corr = lax.all_to_all(corr, CTX, 0, 0)
    grad_k, grad_v, filter_grad = call(
        functools.partial(final_kernel, 1.0 / STRETCH),
        (shape((tok, width), BF16), shape((tok, width), BF16), shape((tok, width), F32)),
        [VMEM] * 5,
    )(corr, grad, keys, values, skip_gain[None, :])
    return grad_q, grad_k, grad_v, filter_grad


COST = 1 << 35


def solution(mesh):
    fine = Mesh(mesh.devices.reshape(4, 8, 2, 4, 2), CTX + TP)
    return jax.shard_map(
        body,
        mesh=fine,
        in_specs=(P(CTX, TP), P(None, TP), P(CTX, TP), P(CTX, TP), P(CTX, TP), P(CTX, TP), P(CTX, TP), P(TP)),
        out_specs=(P(CTX, TP), P(CTX, TP), P(CTX, TP), P(CTX, TP)),
        check_vma=False,
    )
```

```python
import functools
import math

import jax
import jax.numpy as jnp
import numpy as np
from jax import lax
from jax.experimental import pallas as pl
from jax.experimental.pallas import tpu as pltpu
from jax.sharding import Mesh
from jax.sharding import PartitionSpec as P

F32 = jnp.float32
BF16 = jnp.bfloat16
CTX = ("x", "zl")
TP = ("zh", "y", "core")
VMEM = pl.BlockSpec(memory_space=pltpu.VMEM)
SMEM = pl.BlockSpec(memory_space=pltpu.SMEM)
HBM = pl.BlockSpec(memory_space=pltpu.HBM)
STRETCH = 2.0**17
PARAMS = pltpu.CompilerParams(vmem_limit_bytes=16 * 1024 * 1024)


def split_table(table):
    high = table.astype(np.float32).astype(jnp.bfloat16)
    low = (table - high.astype(np.float64)).astype(np.float32).astype(jnp.bfloat16)
    return high, low


def tables(blocks, lanes, chans):
    total = blocks * lanes
    k1 = np.arange(blocks)
    angle = 2.0 * np.pi * np.outer(k1 + 0.25, np.arange(blocks)) / blocks
    eye = np.eye(chans)
    rows = np.concatenate([np.kron(np.cos(angle), eye), np.kron(-np.sin(angle), eye)], axis=0)
    b = np.arange(lanes)
    turn = 2.0 * np.pi * np.outer(k1 + 0.25, b) / total
    twist_re = np.repeat(np.cos(turn), chans, axis=0).astype(np.float32)
    twist_im = np.repeat(-np.sin(turn), chans, axis=0).astype(np.float32)
    lane_angle = 2.0 * np.pi * np.outer(b, b) / lanes
    c, s = np.cos(lane_angle), np.sin(lane_angle)
    lane = np.block([[c, -s], [s, c]])
    return rows, lane, twist_re, twist_im


def lane_dot(x, table):
    high, low = halves(x)
    width = table.shape[1] // 2
    wide = jnp.dot(high, table, preferred_element_type=F32)
    return wide[:, :width] + (wide[:, width:] + jnp.dot(low, table[:, :width], preferred_element_type=F32))


def halves(x):
    high = x.astype(BF16)
    return high, (x - high.astype(F32)).astype(BF16)


def dot3(a, b):
    a_high, a_low = a
    b_high, b_low = b
    dot = functools.partial(jnp.dot, preferred_element_type=F32)
    return dot(a_high, b_high) + (dot(a_high, b_low) + dot(a_low, b_high))


def forward(x, rows, lane, twist_re, twist_im):
    n, lanes = x.shape
    high, low = halves(x)
    both = jnp.dot(rows[0], jnp.concatenate([high, low], axis=1), preferred_element_type=F32)
    first = both[:, :lanes] + (both[:, lanes:] + jnp.dot(rows[1], high, preferred_element_type=F32))
    re, im = first[:n], first[n:]
    turned = jnp.concatenate([re * twist_re - im * twist_im, re * twist_im + im * twist_re], axis=1)
    return lane_dot(turned, lane)


def fetch(pairs, sems):
    copies = [pltpu.make_async_copy(src, dst, sems.at[i]) for i, (src, dst) in enumerate(pairs)]
    for copy in copies:
        copy.start()
    return copies


def prep_kernel(
    scale, filter_hbm, keys_hbm, values_hbm, own_hbm,
    out_hbm, own_ref, out_ref, filter_ref, keys_ref, values_ref, sems,
):
    copies = fetch(
        [(keys_hbm, keys_ref), (values_hbm, values_ref), (filter_hbm, filter_ref), (own_hbm, own_ref)], sems
    )
    blocks, both, lanes = out_ref.shape
    chans = both // 2
    copies[0].wait()
    copies[1].wait()
    gated = keys_ref[...].astype(F32) * values_ref[...].astype(F32)
    out_ref[:, chans:, :] = gated.T.reshape(blocks, chans, lanes)
    first = pltpu.make_async_copy(out_ref.at[:, chans:, :], out_hbm.at[:, chans:, :], sems.at[4])
    first.start()
    copies[2].wait()
    out_ref[:, :chans, :] = (filter_ref[...] * scale).T.reshape(blocks, chans, lanes)
    second = pltpu.make_async_copy(out_ref.at[:, :chans, :], out_hbm.at[:, :chans, :], sems.at[5])
    second.start()
    copies[3].wait()
    first.wait()
    second.wait()


def join_kernel(place_ref, own_ref, far_ref, out_ref):
    zh = place_ref[0]
    out_ref[zh] = own_ref[...]
    out_ref[1 - zh] = far_ref[...]


def products(core, given_ref, proj_ref):
    n_y, n_zh = given_ref.shape[:2]
    total = None
    for y in range(n_y):
        for zh in range(n_zh):
            part = zh * n_y + y
            weights = proj_ref[part] if core is None else proj_ref[part, core]
            term = jnp.dot(given_ref[y, zh], weights, preferred_element_type=F32)
            total = term if total is None else total + term
    return total


def near_kernel(
    place_ref, near_ref, proj_ref, queries_hbm, conv_hbm, part_ref, far_proj_ref, queries_ref, conv_ref, sems
):
    core = place_ref[1]
    copies = fetch([(queries_hbm, queries_ref), (conv_hbm, conv_ref)], sems)
    part_ref[...] = products(core, near_ref, proj_ref)
    for i in range(proj_ref.shape[0]):
        far_proj_ref[i] = proj_ref[i, 1 - core]
    for copy in copies:
        copy.wait()


def spectra_kernel(x_ref, rh, rl, lane, tr, ti, out_ref):
    blocks, both, lanes = x_ref.shape
    chans = both // 2
    for field in range(2):
        x = x_ref[:, field * chans : (field + 1) * chans, :].reshape(blocks * chans, lanes)
        out_ref[field] = forward(x, (rh[...], rl[...]), lane[...], tr[...], ti[...])


def far_kernel(far_ref, part_ref, proj_ref, queries_ref, conv_ref, grad_q_ref, grad_ref, turned_ref):
    total = part_ref[...] + products(None, far_ref, proj_ref)
    grad = total * queries_ref[...].astype(F32)
    turned_ref[...] = grad.T.reshape(turned_ref.shape)
    grad_ref[...] = grad
    grad_q_ref[...] = (total * conv_ref[...].astype(F32)).astype(BF16)


def correlate_kernel(scale, stretch, x_ref, spec_ref, rh, rl, lane, rth, rtl, lt, tr, ti, out_ref):
    blocks, chans, lanes = x_ref.shape
    n = blocks * chans
    twist_re, twist_im = tr[...], ti[...]
    grad = forward(x_ref[...].reshape(n, lanes), (rh[...], rl[...]), lane[...], twist_re, twist_im)
    g_re, g_im = grad[:, :lanes] * scale, grad[:, lanes:] * scale
    sides = []
    for field in range(2):
        s_re, s_im = spec_ref[field, :, :lanes], spec_ref[field, :, lanes:]
        prod = jnp.concatenate([s_re * g_re + s_im * g_im, s_re * g_im - s_im * g_re], axis=1)
        back = lane_dot(prod, lt[...])
        re, im = back[:, :lanes], back[:, lanes:]
        sides.append(jnp.concatenate([re * twist_re + im * twist_im, im * twist_re - re * twist_im], axis=0))
    result = dot3((rth[...], rtl[...]), halves(jnp.concatenate(sides, axis=1)))
    conv, filter_grad = [result[:, f * lanes : (f + 1) * lanes].reshape(blocks, chans, lanes) for f in range(2)]
    high, low = halves(conv)
    stretched = filter_grad * stretch
    cubed = stretched * stretched * stretched
    out_ref[...] = jnp.concatenate([high.astype(F32), low.astype(F32), cubed], axis=1).astype(BF16)


def final_kernel(shrink, x_ref, grad_ref, keys_ref, values_ref, skip_ref, grad_k_ref, grad_v_ref, filter_grad_ref):
    blocks, rows, lanes = x_ref.shape
    chans = rows // 3
    x = x_ref[...].astype(F32)
    conv = (x[:, :chans, :] + x[:, chans : 2 * chans, :]).reshape(blocks * chans, lanes).T
    input_grad = conv + skip_ref[...] * grad_ref[...]
    grad_k_ref[...] = (input_grad * values_ref[...].astype(F32)).astype(BF16)
    grad_v_ref[...] = (input_grad * keys_ref[...].astype(F32)).astype(BF16)
    cubed = x[:, 2 * chans :, :].reshape(blocks * chans, lanes)
    size = jnp.exp2(jnp.log2(jnp.maximum(jnp.abs(cubed), 1e-37)) * (1.0 / 3.0)) * shrink
    root = jnp.where(cubed < 0.0, -size, jnp.where(cubed > 0.0, size, 0.0))
    filter_grad_ref[...] = root.T


def call(kernel, outs, specs, scratch=(), cost=None, out_specs=None):
    run = pl.pallas_call(
        kernel,
        out_shape=outs,
        in_specs=specs,
        out_specs=out_specs or jax.tree.map(lambda _: VMEM, outs),
        scratch_shapes=scratch,
        compiler_params=PARAMS,
        cost_estimate=cost,
    )

    def held(x, spec):
        return pltpu.with_memory_space_constraint(x, pltpu.HBM) if spec is HBM else x

    return lambda *args: run(*map(held, args, specs))


def body(out_grad, out_proj, queries, keys, values, conv_out, long_filter, skip_gain):
    tok, width = queries.shape
    n_ctx = lax.axis_size("x") * lax.axis_size("zl")
    n_half = lax.axis_size("zh") * lax.axis_size("y")
    chans = width // n_ctx
    total_len = tok * n_ctx
    inv_root = 1.0 / math.sqrt(total_len)
    shape = jax.ShapeDtypeStruct
    dma = pltpu.SemaphoreType.DMA

    rows, lane, twist_re, twist_im = tables(n_ctx, tok, chans)
    fwd = [jnp.asarray(t) for t in (*split_table(rows), np.concatenate(split_table(lane), axis=1))]
    inv = [jnp.asarray(t) for t in (*split_table(rows.T), np.concatenate(split_table(lane.T), axis=1))]
    twist = [jnp.asarray(twist_re), jnp.asarray(twist_im)]
    place = jnp.stack([lax.axis_index("zh"), lax.axis_index("core")]).astype(jnp.int32)

    block = shape((tok, width), BF16)
    half = shape((n_half, width, width), BF16)
    proj = out_proj.reshape(n_half, 2, width, width)
    prepared, own = call(
        functools.partial(prep_kernel, inv_root),
        (shape((n_ctx, 2 * chans, tok), F32), block),
        [HBM] * 4,
        [
            pltpu.VMEM((n_ctx, 2 * chans, tok), F32),
            pltpu.VMEM((tok, width), F32),
            pltpu.VMEM((tok, width), BF16),
            pltpu.VMEM((tok, width), BF16),
            dma((6,)),
        ],
        out_specs=(HBM, VMEM),
    )(long_filter, keys, values, out_grad)
    far = lax.ppermute(out_grad, "zh", [(0, 1), (1, 0)])
    fields = lax.all_to_all(prepared, CTX, 0, 0)

    joined = call(
        join_kernel,
        shape((2, tok, width), BF16),
        [SMEM, VMEM, VMEM],
        cost=pl.CostEstimate(flops=COST, bytes_accessed=1 << 20, transcendentals=0),
    )(place, own, far)
    near = lax.all_gather(joined, "y")
    across = lax.ppermute(near, "core", [(0, 1), (1, 0)])
    part, far_proj, gate, saved = call(
        near_kernel,
        (shape((tok, width), F32), half, block, block),
        [SMEM, VMEM, VMEM, HBM, HBM],
        [dma((2,))],
    )(place, near, proj, queries, conv_out)
    across, part = lax.optimization_barrier((across, part))
    grad_q, grad, turned = call(
        far_kernel, (block, shape((tok, width), F32), shape((n_ctx, chans, tok), F32)), [VMEM] * 5
    )(across, part, far_proj, gate, saved)
    turned = lax.all_to_all(turned, CTX, 0, 0)

    spec = call(spectra_kernel, shape((2, n_ctx * chans, 2 * tok), F32), [VMEM] * 6)(fields, *fwd, *twist)
    corr = call(
        functools.partial(correlate_kernel, 1.0 / total_len, inv_root * STRETCH),
        shape((n_ctx, 3 * chans, tok), BF16),
        [VMEM] * 10,
    )(turned, spec, *fwd, *inv, *twist)
    corr = lax.all_to_all(corr, CTX, 0, 0)
    grad_k, grad_v, filter_grad = call(
        functools.partial(final_kernel, 1.0 / STRETCH),
        (shape((tok, width), BF16), shape((tok, width), BF16), shape((tok, width), F32)),
        [VMEM] * 5,
    )(corr, grad, keys, values, skip_gain[None, :])
    return grad_q, grad_k, grad_v, filter_grad


COST = 1 << 35


def solution(mesh):
    fine = Mesh(mesh.devices.reshape(4, 8, 2, 4, 2), CTX + TP)
    return jax.shard_map(
        body,
        mesh=fine,
        in_specs=(P(CTX, TP), P(None, TP), P(CTX, TP), P(CTX, TP), P(CTX, TP), P(CTX, TP), P(CTX, TP), P(TP)),
        out_specs=(P(CTX, TP), P(CTX, TP), P(CTX, TP), P(CTX, TP)),
        check_vma=False,
    )
```

```python
import functools
import math

import jax
import jax.numpy as jnp
import numpy as np
from jax import lax
from jax.experimental import pallas as pl
from jax.experimental.pallas import tpu as pltpu
from jax.sharding import Mesh
from jax.sharding import PartitionSpec as P

F32 = jnp.float32
BF16 = jnp.bfloat16
CTX = ("x", "zl")
TP = ("zh", "y", "core")
VMEM = pl.BlockSpec(memory_space=pltpu.VMEM)
SMEM = pl.BlockSpec(memory_space=pltpu.SMEM)
HBM = pl.BlockSpec(memory_space=pltpu.HBM)
STRETCH = 2.0**17
PARAMS = pltpu.CompilerParams(vmem_limit_bytes=16 * 1024 * 1024)


def split_table(table):
    high = table.astype(np.float32).astype(jnp.bfloat16)
    low = (table - high.astype(np.float64)).astype(np.float32).astype(jnp.bfloat16)
    return high, low


def tables(blocks, lanes, chans):
    total = blocks * lanes
    k1 = np.arange(blocks)
    angle = 2.0 * np.pi * np.outer(k1 + 0.25, np.arange(blocks)) / blocks
    eye = np.eye(chans)
    rows = np.concatenate([np.kron(np.cos(angle), eye), np.kron(-np.sin(angle), eye)], axis=0)
    b = np.arange(lanes)
    turn = 2.0 * np.pi * np.outer(k1 + 0.25, b) / total
    twist_re = np.repeat(np.cos(turn), chans, axis=0).astype(np.float32)
    twist_im = np.repeat(-np.sin(turn), chans, axis=0).astype(np.float32)
    lane_angle = 2.0 * np.pi * np.outer(b, b) / lanes
    c, s = np.cos(lane_angle), np.sin(lane_angle)
    lane = np.block([[c, -s], [s, c]])
    return rows, lane, twist_re, twist_im


def halves(x):
    high = x.astype(BF16)
    return high, (x - high.astype(F32)).astype(BF16)


def dot3(a, b):
    a_high, a_low = a
    b_high, b_low = b
    dot = functools.partial(jnp.dot, preferred_element_type=F32)
    return dot(a_high, b_high) + (dot(a_high, b_low) + dot(a_low, b_high))


def forward(x, rows, lane, twist_re, twist_im):
    n, lanes = x.shape
    high, low = halves(x)
    both = jnp.dot(rows[0], jnp.concatenate([high, low], axis=1), preferred_element_type=F32)
    first = both[:, :lanes] + (both[:, lanes:] + jnp.dot(rows[1], high, preferred_element_type=F32))
    re, im = first[:n], first[n:]
    turned = jnp.concatenate([re * twist_re - im * twist_im, re * twist_im + im * twist_re], axis=1)
    return dot3(halves(turned), lane)


def fetch(pairs, sems):
    copies = [pltpu.make_async_copy(src, dst, sems.at[i]) for i, (src, dst) in enumerate(pairs)]
    for copy in copies:
        copy.start()
    return copies


def prep_kernel(
    scale, filter_hbm, keys_hbm, values_hbm, own_hbm,
    out_hbm, own_ref, out_ref, filter_ref, keys_ref, values_ref, sems,
):
    copies = fetch(
        [(keys_hbm, keys_ref), (values_hbm, values_ref), (filter_hbm, filter_ref), (own_hbm, own_ref)], sems
    )
    blocks, both, lanes = out_ref.shape
    chans = both // 2
    copies[0].wait()
    copies[1].wait()
    gated = keys_ref[...].astype(F32) * values_ref[...].astype(F32)
    out_ref[:, chans:, :] = gated.T.reshape(blocks, chans, lanes)
    first = pltpu.make_async_copy(out_ref.at[:, chans:, :], out_hbm.at[:, chans:, :], sems.at[4])
    first.start()
    copies[2].wait()
    out_ref[:, :chans, :] = (filter_ref[...] * scale).T.reshape(blocks, chans, lanes)
    second = pltpu.make_async_copy(out_ref.at[:, :chans, :], out_hbm.at[:, :chans, :], sems.at[5])
    second.start()
    copies[3].wait()
    first.wait()
    second.wait()


def products(core, given_ref, proj_ref):
    n_y, n_zh = given_ref.shape[:2]
    total = None
    for y in range(n_y):
        for zh in range(n_zh):
            part = zh * n_y + y
            weights = proj_ref[part] if core is None else proj_ref[part, core]
            term = jnp.dot(given_ref[y, zh], weights, preferred_element_type=F32)
            total = term if total is None else total + term
    return total


def near_kernel(
    place_ref, near_ref, proj_ref, queries_hbm, conv_hbm, part_ref, far_proj_ref, queries_ref, conv_ref, sems
):
    core = place_ref[1]
    copies = fetch([(queries_hbm, queries_ref), (conv_hbm, conv_ref)], sems)
    part_ref[...] = products(core, near_ref, proj_ref)
    for i in range(proj_ref.shape[0]):
        far_proj_ref[i] = proj_ref[i, 1 - core]
    for copy in copies:
        copy.wait()


def spectra_kernel(x_ref, rh, rl, lh, ll, tr, ti, out_ref):
    blocks, both, lanes = x_ref.shape
    chans = both // 2
    for field in range(2):
        x = x_ref[:, field * chans : (field + 1) * chans, :].reshape(blocks * chans, lanes)
        out_ref[field] = forward(x, (rh[...], rl[...]), (lh[...], ll[...]), tr[...], ti[...])


def far_kernel(far_ref, part_ref, proj_ref, queries_ref, conv_ref, grad_q_ref, grad_ref, turned_ref):
    total = part_ref[...] + products(None, far_ref, proj_ref)
    grad = total * queries_ref[...].astype(F32)
    turned_ref[...] = grad.T.reshape(turned_ref.shape)
    grad_ref[...] = grad
    grad_q_ref[...] = (total * conv_ref[...].astype(F32)).astype(BF16)


def correlate_kernel(scale, stretch, x_ref, spec_ref, rh, rl, lh, ll, rth, rtl, lth, ltl, tr, ti, out_ref):
    blocks, chans, lanes = x_ref.shape
    n = blocks * chans
    twist_re, twist_im = tr[...], ti[...]
    grad = forward(x_ref[...].reshape(n, lanes), (rh[...], rl[...]), (lh[...], ll[...]), twist_re, twist_im)
    g_re, g_im = grad[:, :lanes] * scale, grad[:, lanes:] * scale
    sides = []
    for field in range(2):
        s_re, s_im = spec_ref[field, :, :lanes], spec_ref[field, :, lanes:]
        prod = jnp.concatenate([s_re * g_re + s_im * g_im, s_re * g_im - s_im * g_re], axis=1)
        back = dot3(halves(prod), (lth[...], ltl[...]))
        re, im = back[:, :lanes], back[:, lanes:]
        sides.append(jnp.concatenate([re * twist_re + im * twist_im, im * twist_re - re * twist_im], axis=0))
    result = dot3((rth[...], rtl[...]), halves(jnp.concatenate(sides, axis=1)))
    conv, filter_grad = [result[:, f * lanes : (f + 1) * lanes].reshape(blocks, chans, lanes) for f in range(2)]
    high, low = halves(conv)
    stretched = filter_grad * stretch
    cubed = stretched * stretched * stretched
    out_ref[...] = jnp.concatenate([high.astype(F32), low.astype(F32), cubed], axis=1).astype(BF16)


def final_kernel(shrink, x_ref, grad_ref, keys_ref, values_ref, skip_ref, grad_k_ref, grad_v_ref, filter_grad_ref):
    blocks, rows, lanes = x_ref.shape
    chans = rows // 3
    x = x_ref[...].astype(F32)
    conv = (x[:, :chans, :] + x[:, chans : 2 * chans, :]).reshape(blocks * chans, lanes).T
    input_grad = conv + skip_ref[...] * grad_ref[...]
    grad_k_ref[...] = (input_grad * values_ref[...].astype(F32)).astype(BF16)
    grad_v_ref[...] = (input_grad * keys_ref[...].astype(F32)).astype(BF16)
    cubed = x[:, 2 * chans :, :].reshape(blocks * chans, lanes)
    size = jnp.exp2(jnp.log2(jnp.maximum(jnp.abs(cubed), 1e-37)) * (1.0 / 3.0)) * shrink
    root = jnp.where(cubed < 0.0, -size, jnp.where(cubed > 0.0, size, 0.0))
    filter_grad_ref[...] = root.T


def call(kernel, outs, specs, scratch=(), cost=None, out_specs=None):
    run = pl.pallas_call(
        kernel,
        out_shape=outs,
        in_specs=specs,
        out_specs=out_specs or jax.tree.map(lambda _: VMEM, outs),
        scratch_shapes=scratch,
        compiler_params=PARAMS,
        cost_estimate=cost,
    )

    def held(x, spec):
        return pltpu.with_memory_space_constraint(x, pltpu.HBM) if spec is HBM else x

    return lambda *args: run(*map(held, args, specs))


def body(out_grad, out_proj, queries, keys, values, conv_out, long_filter, skip_gain):
    tok, width = queries.shape
    n_ctx = lax.axis_size("x") * lax.axis_size("zl")
    n_half = lax.axis_size("zh") * lax.axis_size("y")
    chans = width // n_ctx
    total_len = tok * n_ctx
    inv_root = 1.0 / math.sqrt(total_len)
    shape = jax.ShapeDtypeStruct
    dma = pltpu.SemaphoreType.DMA

    rows, lane, twist_re, twist_im = tables(n_ctx, tok, chans)
    fwd = [jnp.asarray(t) for t in (*split_table(rows), *split_table(lane))]
    inv = [jnp.asarray(t) for t in (*split_table(rows.T), *split_table(lane.T))]
    twist = [jnp.asarray(twist_re), jnp.asarray(twist_im)]
    place = jnp.stack([lax.axis_index("zh"), lax.axis_index("core")]).astype(jnp.int32)

    block = shape((tok, width), BF16)
    half = shape((n_half, width, width), BF16)
    proj = out_proj.reshape(n_half, 2, width, width)
    prepared, own = call(
        functools.partial(prep_kernel, inv_root),
        (shape((n_ctx, 2 * chans, tok), F32), block),
        [HBM] * 4,
        [
            pltpu.VMEM((n_ctx, 2 * chans, tok), F32),
            pltpu.VMEM((tok, width), F32),
            pltpu.VMEM((tok, width), BF16),
            pltpu.VMEM((tok, width), BF16),
            dma((6,)),
        ],
        cost=pl.CostEstimate(flops=COST, bytes_accessed=1 << 20, transcendentals=0),
        out_specs=(HBM, VMEM),
    )(long_filter, keys, values, out_grad)
    far = lax.ppermute(own, "zh", [(0, 1), (1, 0)])
    fields = lax.all_to_all(prepared, CTX, 0, 0)

    upper = lax.axis_index("zh") == 1
    joined = jnp.stack([jnp.where(upper, far, own), jnp.where(upper, own, far)])
    near = lax.all_gather(joined, "y")
    across = lax.ppermute(near, "core", [(0, 1), (1, 0)])
    part, far_proj, gate, saved = call(
        near_kernel,
        (shape((tok, width), F32), half, block, block),
        [SMEM, VMEM, VMEM, HBM, HBM],
        [dma((2,))],
        cost=pl.CostEstimate(flops=COST, bytes_accessed=1 << 20, transcendentals=0),
    )(place, near, proj, queries, conv_out)
    across, part = lax.optimization_barrier((across, part))
    grad_q, grad, turned = call(
        far_kernel, (block, shape((tok, width), F32), shape((n_ctx, chans, tok), F32)), [VMEM] * 5
    )(across, part, far_proj, gate, saved)
    turned = lax.all_to_all(turned, CTX, 0, 0)

    spec = call(spectra_kernel, shape((2, n_ctx * chans, 2 * tok), F32), [VMEM] * 7)(fields, *fwd, *twist)
    corr = call(
        functools.partial(correlate_kernel, 1.0 / total_len, inv_root * STRETCH),
        shape((n_ctx, 3 * chans, tok), BF16),
        [VMEM] * 12,
    )(turned, spec, *fwd, *inv, *twist)
    corr = lax.all_to_all(corr, CTX, 0, 0)
    grad_k, grad_v, filter_grad = call(
        functools.partial(final_kernel, 1.0 / STRETCH),
        (shape((tok, width), BF16), shape((tok, width), BF16), shape((tok, width), F32)),
        [VMEM] * 5,
    )(corr, grad, keys, values, skip_gain[None, :])
    return grad_q, grad_k, grad_v, filter_grad


COST = 1 << 35


def solution(mesh):
    fine = Mesh(mesh.devices.reshape(4, 8, 2, 4, 2), CTX + TP)
    return jax.shard_map(
        body,
        mesh=fine,
        in_specs=(P(CTX, TP), P(None, TP), P(CTX, TP), P(CTX, TP), P(CTX, TP), P(CTX, TP), P(CTX, TP), P(TP)),
        out_specs=(P(CTX, TP), P(CTX, TP), P(CTX, TP), P(CTX, TP)),
        check_vma=False,
    )
```

```python
import functools
import math

import jax
import jax.numpy as jnp
import numpy as np
from jax import lax
from jax.experimental import pallas as pl
from jax.experimental.pallas import tpu as pltpu
from jax.sharding import Mesh
from jax.sharding import PartitionSpec as P

F32 = jnp.float32
BF16 = jnp.bfloat16
CTX = ("x", "zl")
TP = ("zh", "y", "core")
VMEM = pl.BlockSpec(memory_space=pltpu.VMEM)
SMEM = pl.BlockSpec(memory_space=pltpu.SMEM)
HBM = pl.BlockSpec(memory_space=pltpu.HBM)
STRETCH = 2.0**17
PARAMS = pltpu.CompilerParams(vmem_limit_bytes=16 * 1024 * 1024)


def split_table(table):
    high = table.astype(np.float32).astype(jnp.bfloat16)
    low = (table - high.astype(np.float64)).astype(np.float32).astype(jnp.bfloat16)
    return high, low


def tables(blocks, lanes, chans):
    total = blocks * lanes
    k1 = np.arange(blocks)
    angle = 2.0 * np.pi * np.outer(k1 + 0.25, np.arange(blocks)) / blocks
    eye = np.eye(chans)
    rows = np.concatenate([np.kron(np.cos(angle), eye), np.kron(-np.sin(angle), eye)], axis=0)
    b = np.arange(lanes)
    turn = 2.0 * np.pi * np.outer(k1 + 0.25, b) / total
    twist_re = np.repeat(np.cos(turn), chans, axis=0).astype(np.float32)
    twist_im = np.repeat(-np.sin(turn), chans, axis=0).astype(np.float32)
    lane_angle = 2.0 * np.pi * np.outer(b, b) / lanes
    c, s = np.cos(lane_angle), np.sin(lane_angle)
    lane = np.block([[c, -s], [s, c]])
    return rows, lane, twist_re, twist_im


def halves(x):
    high = x.astype(BF16)
    return high, (x - high.astype(F32)).astype(BF16)


def dot3(a, b):
    a_high, a_low = a
    b_high, b_low = b
    dot = functools.partial(jnp.dot, preferred_element_type=F32)
    return dot(a_high, b_high) + (dot(a_high, b_low) + dot(a_low, b_high))


def forward(x, rows, lane, twist_re, twist_im):
    n, lanes = x.shape
    high, low = halves(x)
    both = jnp.dot(rows[0], jnp.concatenate([high, low], axis=1), preferred_element_type=F32)
    first = both[:, :lanes] + (both[:, lanes:] + jnp.dot(rows[1], high, preferred_element_type=F32))
    re, im = first[:n], first[n:]
    turned = jnp.concatenate([re * twist_re - im * twist_im, re * twist_im + im * twist_re], axis=1)
    return dot3(halves(turned), lane)


def fetch(pairs, sems):
    copies = [pltpu.make_async_copy(src, dst, sems.at[i]) for i, (src, dst) in enumerate(pairs)]
    for copy in copies:
        copy.start()
    return copies


def prep_kernel(
    scale, filter_hbm, keys_hbm, values_hbm, own_hbm,
    out_hbm, own_ref, out_ref, filter_ref, keys_ref, values_ref, sems,
):
    copies = fetch(
        [(keys_hbm, keys_ref), (values_hbm, values_ref), (filter_hbm, filter_ref), (own_hbm, own_ref)], sems
    )
    blocks, both, lanes = out_ref.shape
    chans = both // 2
    copies[0].wait()
    copies[1].wait()
    gated = keys_ref[...].astype(F32) * values_ref[...].astype(F32)
    out_ref[:, chans:, :] = gated.T.reshape(blocks, chans, lanes)
    first = pltpu.make_async_copy(out_ref.at[:, chans:, :], out_hbm.at[:, chans:, :], sems.at[4])
    first.start()
    copies[2].wait()
    out_ref[:, :chans, :] = (filter_ref[...] * scale).T.reshape(blocks, chans, lanes)
    second = pltpu.make_async_copy(out_ref.at[:, :chans, :], out_hbm.at[:, :chans, :], sems.at[5])
    second.start()
    copies[3].wait()
    first.wait()
    second.wait()


def products(core, given_ref, proj_ref):
    n_y, n_zh = given_ref.shape[:2]
    total = None
    for y in range(n_y):
        for zh in range(n_zh):
            part = zh * n_y + y
            weights = proj_ref[part] if core is None else proj_ref[part, core]
            term = jnp.dot(given_ref[y, zh], weights, preferred_element_type=F32)
            total = term if total is None else total + term
    return total


def near_kernel(
    place_ref, near_ref, proj_ref, queries_hbm, conv_hbm, part_ref, far_proj_ref, queries_ref, conv_ref, sems
):
    core = place_ref[1]
    copies = fetch([(queries_hbm, queries_ref), (conv_hbm, conv_ref)], sems)
    part_ref[...] = products(core, near_ref, proj_ref)
    for i in range(proj_ref.shape[0]):
        far_proj_ref[i] = proj_ref[i, 1 - core]
    for copy in copies:
        copy.wait()


def spectra_kernel(x_ref, rh, rl, lh, ll, tr, ti, out_ref):
    blocks, both, lanes = x_ref.shape
    chans = both // 2
    for field in range(2):
        x = x_ref[:, field * chans : (field + 1) * chans, :].reshape(blocks * chans, lanes)
        out_ref[field] = forward(x, (rh[...], rl[...]), (lh[...], ll[...]), tr[...], ti[...])


def far_kernel(far_ref, part_ref, proj_ref, queries_ref, conv_ref, grad_q_ref, grad_ref, turned_ref):
    total = part_ref[...] + products(None, far_ref, proj_ref)
    grad = total * queries_ref[...].astype(F32)
    turned_ref[...] = grad.T.reshape(turned_ref.shape)
    grad_ref[...] = grad
    grad_q_ref[...] = (total * conv_ref[...].astype(F32)).astype(BF16)


def correlate_kernel(scale, stretch, x_ref, spec_ref, rh, rl, lh, ll, rth, rtl, lth, ltl, tr, ti, out_ref):
    blocks, chans, lanes = x_ref.shape
    n = blocks * chans
    twist_re, twist_im = tr[...], ti[...]
    grad = forward(x_ref[...].reshape(n, lanes), (rh[...], rl[...]), (lh[...], ll[...]), twist_re, twist_im)
    g_re, g_im = grad[:, :lanes] * scale, grad[:, lanes:] * scale
    sides = []
    for field in range(2):
        s_re, s_im = spec_ref[field, :, :lanes], spec_ref[field, :, lanes:]
        prod = jnp.concatenate([s_re * g_re + s_im * g_im, s_re * g_im - s_im * g_re], axis=1)
        back = dot3(halves(prod), (lth[...], ltl[...]))
        re, im = back[:, :lanes], back[:, lanes:]
        sides.append(jnp.concatenate([re * twist_re + im * twist_im, im * twist_re - re * twist_im], axis=0))
    result = dot3((rth[...], rtl[...]), halves(jnp.concatenate(sides, axis=1)))
    conv, filter_grad = [result[:, f * lanes : (f + 1) * lanes].reshape(blocks, chans, lanes) for f in range(2)]
    high, low = halves(conv)
    stretched = filter_grad * stretch
    cubed = stretched * stretched * stretched
    out_ref[...] = jnp.concatenate([high.astype(F32), low.astype(F32), cubed], axis=1).astype(BF16)


def final_kernel(shrink, x_ref, grad_ref, keys_ref, values_ref, skip_ref, grad_k_ref, grad_v_ref, filter_grad_ref):
    blocks, rows, lanes = x_ref.shape
    chans = rows // 3
    x = x_ref[...].astype(F32)
    conv = (x[:, :chans, :] + x[:, chans : 2 * chans, :]).reshape(blocks * chans, lanes).T
    input_grad = conv + skip_ref[...] * grad_ref[...]
    grad_k_ref[...] = (input_grad * values_ref[...].astype(F32)).astype(BF16)
    grad_v_ref[...] = (input_grad * keys_ref[...].astype(F32)).astype(BF16)
    cubed = x[:, 2 * chans :, :].reshape(blocks * chans, lanes)
    size = jnp.exp2(jnp.log2(jnp.maximum(jnp.abs(cubed), 1e-37)) * (1.0 / 3.0)) * shrink
    root = jnp.where(cubed < 0.0, -size, jnp.where(cubed > 0.0, size, 0.0))
    filter_grad_ref[...] = root.T


def call(kernel, outs, specs, scratch=(), cost=None, out_specs=None):
    run = pl.pallas_call(
        kernel,
        out_shape=outs,
        in_specs=specs,
        out_specs=out_specs or jax.tree.map(lambda _: VMEM, outs),
        scratch_shapes=scratch,
        compiler_params=PARAMS,
        cost_estimate=cost,
    )

    def held(x, spec):
        return pltpu.with_memory_space_constraint(x, pltpu.HBM) if spec is HBM else x

    return lambda *args: run(*map(held, args, specs))


def body(out_grad, out_proj, queries, keys, values, conv_out, long_filter, skip_gain):
    tok, width = queries.shape
    n_ctx = lax.axis_size("x") * lax.axis_size("zl")
    n_half = lax.axis_size("zh") * lax.axis_size("y")
    chans = width // n_ctx
    total_len = tok * n_ctx
    inv_root = 1.0 / math.sqrt(total_len)
    shape = jax.ShapeDtypeStruct
    dma = pltpu.SemaphoreType.DMA

    rows, lane, twist_re, twist_im = tables(n_ctx, tok, chans)
    fwd = [jnp.asarray(t) for t in (*split_table(rows), *split_table(lane))]
    inv = [jnp.asarray(t) for t in (*split_table(rows.T), *split_table(lane.T))]
    twist = [jnp.asarray(twist_re), jnp.asarray(twist_im)]
    place = jnp.stack([lax.axis_index("zh"), lax.axis_index("core")]).astype(jnp.int32)

    block = shape((tok, width), BF16)
    half = shape((n_half, width, width), BF16)
    proj = out_proj.reshape(n_half, 2, width, width)
    prepared, own = call(
        functools.partial(prep_kernel, inv_root),
        (shape((n_ctx, 2 * chans, tok), F32), block),
        [HBM] * 4,
        [
            pltpu.VMEM((n_ctx, 2 * chans, tok), F32),
            pltpu.VMEM((tok, width), F32),
            pltpu.VMEM((tok, width), BF16),
            pltpu.VMEM((tok, width), BF16),
            dma((6,)),
        ],
        cost=pl.CostEstimate(flops=COST, bytes_accessed=1 << 20, transcendentals=0),
        out_specs=(HBM, VMEM),
    )(long_filter, keys, values, out_grad)
    far = lax.ppermute(out_grad, "zh", [(0, 1), (1, 0)])
    fields = lax.all_to_all(prepared, CTX, 0, 0)

    upper = lax.axis_index("zh") == 1
    joined = jnp.stack([jnp.where(upper, far, own), jnp.where(upper, own, far)])
    near = lax.all_gather(joined, "y")
    across = lax.ppermute(near, "core", [(0, 1), (1, 0)])
    part, far_proj, gate, saved = call(
        near_kernel,
        (shape((tok, width), F32), half, block, block),
        [SMEM, VMEM, VMEM, HBM, HBM],
        [dma((2,))],
        cost=pl.CostEstimate(flops=COST, bytes_accessed=1 << 20, transcendentals=0),
    )(place, near, proj, queries, conv_out)
    across, part = lax.optimization_barrier((across, part))
    grad_q, grad, turned = call(
        far_kernel, (block, shape((tok, width), F32), shape((n_ctx, chans, tok), F32)), [VMEM] * 5
    )(across, part, far_proj, gate, saved)
    turned = lax.all_to_all(turned, CTX, 0, 0)

    spec = call(spectra_kernel, shape((2, n_ctx * chans, 2 * tok), F32), [VMEM] * 7)(fields, *fwd, *twist)
    corr = call(
        functools.partial(correlate_kernel, 1.0 / total_len, inv_root * STRETCH),
        shape((n_ctx, 3 * chans, tok), BF16),
        [VMEM] * 12,
    )(turned, spec, *fwd, *inv, *twist)
    corr = lax.all_to_all(corr, CTX, 0, 0)
    grad_k, grad_v, filter_grad = call(
        functools.partial(final_kernel, 1.0 / STRETCH),
        (shape((tok, width), BF16), shape((tok, width), BF16), shape((tok, width), F32)),
        [VMEM] * 5,
    )(corr, grad, keys, values, skip_gain[None, :])
    return grad_q, grad_k, grad_v, filter_grad


COST = 1 << 35


def solution(mesh):
    fine = Mesh(mesh.devices.reshape(4, 8, 2, 4, 2), CTX + TP)
    return jax.shard_map(
        body,
        mesh=fine,
        in_specs=(P(CTX, TP), P(None, TP), P(CTX, TP), P(CTX, TP), P(CTX, TP), P(CTX, TP), P(CTX, TP), P(TP)),
        out_specs=(P(CTX, TP), P(CTX, TP), P(CTX, TP), P(CTX, TP)),
        check_vma=False,
    )
```
